512 devices in a mesh: gz: 32 (over z, core), gy: 4 (over y), gx: 4 (over x).
Axes of the slice: x: 4, y: 4, z: 16, core: 2. Of those that a mesh axis runs over, the one named last changes fastest.
Arguments:
- pressure: float32 [128, 512, 512], P('gz', 'gy', 'gx'), may hold values from -6 to 6
- light: float32 [4, 3], replicated, may hold values from -4 to 4
- palette: float32 [3, 2], replicated, may hold values from -4 to 4
- rate: float32 [4], replicated, may hold values from 0.00390625 to 0.0234375
- shear: int32 [4, 128, 2], replicated, may hold values from 0 to 8
- offset: int32 [4, 32, 2], replicated, may hold values from 0 to 31
- order: int32 [4, 32], replicated, may hold values from 0 to 31, each once within a row
Outputs:
- picture: float32 [4, 4, 32, 16, 512], P(None, None, 'gz', 'gy', 'gx')
The draws below stay inside these ranges and needn't reach their ends.
Inputs may be any that keep to these rules, and one draw needn't show every extreme that they name: `order`: each row is a permutation of 0 to 31.
All inputs are finite; a program needn't handle non-finite values.
Results may differ from the reference program's by a relative error of at most 0.00005.
Values sent between devices are 32-bit elements; how exact they have to be, the bound alone decides.
No kernel may reach another device: no remote copies, remote signals or barrier semaphores. Data moves between devices by JAX's collectives and lax.ppermute only.
A program may use at most 64 MiB of HBM per device.

```python
import math
import jax
import jax.numpy as jnp
from jax import lax

BZ = 4
VIEWS = 4
SHEAR = 8
REACH = 32
NBRICK = 32
NZ = 128
NY = 512
NX = 512
ROWS = 4
N_GY = 4


def draw_shear(key, part):
    drawn = jax.random.randint(jax.random.fold_in(key, 11), (VIEWS, NZ, 2), 0, SHEAR + 1)
    picked = jax.random.randint(jax.random.fold_in(key, 12), (VIEWS,), 0, NZ)
    marked = (jnp.arange(NZ, dtype=jnp.int32)[None, :] == picked[:, None])[:, :, None]
    return jnp.where(marked, SHEAR, drawn).astype(jnp.int32)


def draw_offset(key, part):
    drawn = jax.random.randint(jax.random.fold_in(key, 21), (VIEWS, NBRICK, 2), 0, REACH)
    picked = jax.random.randint(jax.random.fold_in(key, 22), (VIEWS,), 0, NBRICK)
    marked = (jnp.arange(NBRICK, dtype=jnp.int32)[None, :] == picked[:, None])[:, :, None]
    return jnp.where(marked, REACH - 1, drawn).astype(jnp.int32)


def block_levels(own_key, shape, split, low, high):
    def one(axis_at, shards_of):
        steps = jax.random.uniform(jax.random.fold_in(jax.random.fold_in(own_key, 6), axis_at), (shards_of,), jnp.float32, low / len(split), high / len(split))
        return jnp.repeat(jnp.exp(steps), shape[axis_at] // shards_of).reshape((-1,) + (1,) * (len(shape) - axis_at - 1))

    factor_of = one(*split[0])
    for cut in split[1:]:
        factor_of = factor_of * one(*cut)
    return factor_of


def bell_draw(stream_key, extent, spread, limit, split=(), kind=jnp.bfloat16):
    gain = block_levels(stream_key, extent, split, -0.22, 0.18) if split else 1.0
    result = jax.random.normal(stream_key, extent, jnp.float32) * spread * gain
    return jnp.minimum(jnp.maximum(result, -limit), limit).astype(kind)


def setup_inputs(seed: int = 0) -> dict:
    seeds = jax.random.split(jax.random.key(seed), 8)
    pressure = bell_draw(seeds[0], (NZ, NY, NX), 1.0, 6.0, ((0, 32), (1, 4), (2, 4)), jnp.float32)
    light = bell_draw(seeds[1], (VIEWS, 3), 1.0, 4.0, (), jnp.float32)
    palette = bell_draw(seeds[2], (3, 2), 1.0, 4.0, (), jnp.float32)
    rate = jnp.clip(jnp.exp(jax.random.uniform(seeds[3], (VIEWS,), jnp.float32, math.log(0.00390625), math.log(0.0234375))), 0.00390625, 0.0234375)
    shear = draw_shear(jax.random.fold_in(seeds[7], 71), 0)
    offset = draw_offset(jax.random.fold_in(seeds[7], 71), 0)
    order = jax.vmap(lambda own: jax.random.permutation(own, NBRICK))(jax.random.split(seeds[6], VIEWS)).reshape((VIEWS, NBRICK)).astype(jnp.int32)
    return dict(pressure=pressure, light=light, palette=palette, rate=rate, shear=shear, offset=offset, order=order)


def surface_terms(slab):
    inner = slab[1:-1, 1:-1, 1:-1]
    grad_depth = 0.5 * (slab[2:, 1:-1, 1:-1] - slab[:-2, 1:-1, 1:-1])
    grad_rows = 0.5 * (slab[1:-1, 2:, 1:-1] - slab[1:-1, :-2, 1:-1])
    grad_cols = 0.5 * (slab[1:-1, 1:-1, 2:] - slab[1:-1, 1:-1, :-2])
    factor = lax.rsqrt(grad_depth * grad_depth + grad_rows * grad_rows + grad_cols * grad_cols + 1.0)
    return (inner, (grad_depth * factor, grad_rows * factor, grad_cols * factor))

def render_layers(inner, normals, shifts, light, palette, rate, rows, cols):
    lengths = jnp.sqrt(lax.optimization_barrier(jnp.sum(light * light, axis=1, keepdims=True)) + 1.0)
    towards = light / lengths
    offsets = palette[:, 0][:, None, None]
    slopes = palette[:, 1][:, None, None]
    layers = []
    for view in range(light.shape[0]):

        def advance(carry, items):
            color, depth = carry
            value_slab, normal_depth, normal_rows, normal_cols, moved = items
            start = (SHEAR - moved[0], SHEAR - moved[1])
            value = lax.dynamic_slice(value_slab, start, (rows, cols))
            dot = lax.dynamic_slice(normal_depth, start, (rows, cols)) * towards[view, 0] + lax.dynamic_slice(normal_rows, start, (rows, cols)) * towards[view, 1] + lax.dynamic_slice(normal_cols, start, (rows, cols)) * towards[view, 2]
            shade = 0.25 + 0.75 * dot * dot
            density = rate[view] * (1.0 + jnp.tanh(value))
            alpha = 1.0 - jnp.exp(-density)
            weight = alpha * jnp.exp(-depth)
            hues = jax.nn.sigmoid(offsets + slopes * value[None]) * shade[None]
            return ((color + hues * weight[None], depth + density), None)
        start_carry = (jnp.zeros((3, rows, cols), jnp.float32), jnp.zeros((rows, cols), jnp.float32))
        (color, depth), _ = lax.scan(advance, start_carry, (inner, normals[0], normals[1], normals[2], shifts[view]))
        layers.append(jnp.concatenate([color, depth[None]], axis=0))
    return jnp.stack(layers)

def precedence(order):
    bricks = order.shape[1]
    onehot = (order[:, :, None] == jnp.arange(bricks, dtype=jnp.int32)[None, None, :]).astype(jnp.float32)
    ranks = lax.optimization_barrier(jnp.sum(onehot * jnp.arange(bricks, dtype=jnp.float32)[None, :, None], axis=1))
    return (ranks[:, None, :] < ranks[:, :, None]).astype(jnp.float32)

def place(layer, moved):
    padded = jnp.pad(layer, ((0, 0), (REACH, 0), (REACH, 0)))
    zero = jnp.zeros((), jnp.int32)
    return lax.dynamic_slice(padded, (zero, REACH - moved[0], REACH - moved[1]), layer.shape)

def reference(pressure, light, palette, rate, shear, offset, order):
    margin = SHEAR + 1
    rows = pressure.shape[1]
    cols = pressure.shape[2]
    padded = jnp.pad(pressure, ((1, 1), (margin, margin), (margin, margin)))

    def one_brick(brick):
        zero = jnp.zeros((), jnp.int32)
        slab = lax.dynamic_slice(padded, (brick * BZ, zero, zero), (BZ + 2, rows + 2 * margin, cols + 2 * margin))
        inner, normals = surface_terms(slab)
        shifts = lax.dynamic_slice(shear, (zero, brick * BZ, zero), (VIEWS, BZ, 2))
        layers = render_layers(inner, normals, shifts, light, palette, rate, rows, cols)
        moved = lax.dynamic_index_in_dim(offset, brick, 1, keepdims=False)
        return jnp.stack([place(layers[view], moved[view]) for view in range(VIEWS)])
    stacked = lax.map(one_brick, jnp.arange(NBRICK, dtype=jnp.int32))
    ranking = precedence(order)
    depths = stacked[:, :, 3]
    cover = jnp.einsum('vbc,cvyx->bvyx', ranking, depths, precision=lax.Precision.HIGHEST)
    colors = lax.optimization_barrier(jnp.sum(stacked[:, :, :3] * jnp.exp(-cover)[:, :, None], axis=0))
    opacity = 1.0 - jnp.exp(-lax.optimization_barrier(jnp.sum(depths, axis=0)))
    image = jnp.concatenate([colors, opacity[:, None]], axis=1)
    image = image.reshape(VIEWS, 4, N_GY, NBRICK, ROWS, NX)
    image = jnp.transpose(image, (0, 1, 3, 2, 4, 5))
    return image.reshape(VIEWS, 4, NBRICK, N_GY * ROWS, NX)
```

```python
import functools

import jax
import jax.numpy as jnp
from jax import lax
from jax.experimental import pallas as pl
from jax.experimental.pallas import tpu as pltpu
from jax.sharding import PartitionSpec as P

VIEWS = 4
BZ = 4
TILE = 128
HALO = 40
EXT = HALO + TILE
BASE = 8
CHUNK = 16

VMEM = pl.BlockSpec(memory_space=pltpu.VMEM)
SMEM = pl.BlockSpec(memory_space=pltpu.SMEM)


def render_kernel(
    moves_ref, light_ref, palette_ref, rate_ref,
    own_ref, above_ref, left_ref, corner_ref, front_ref, back_ref, below_ref, right_ref,
    out_ref,
    core_s, side_s, near_s, fields,
):
    gy = lax.axis_index("gy")
    gx = lax.axis_index("gx")
    lane8 = lax.broadcasted_iota(jnp.int32, (8, TILE), 1)

    for k in range(BZ):
        core_s[k, BASE : BASE + HALO] = above_ref[k]
        core_s[k, BASE + HALO : BASE + EXT] = own_ref[k]
        core_s[k, BASE + EXT : BASE + EXT + 1] = below_ref[k : k + 1]
        pack = 0 if k in (0, 3) else 1
        corner, left, below = corner_ref[pack], left_ref[pack], below_ref[4 + pack : 5 + pack]
        if k >= 2:
            corner = pltpu.roll(corner, 64, axis=1)
            left = pltpu.roll(left, 64, axis=1)
            below = pltpu.roll(jnp.broadcast_to(below, (8, TILE)), 64, axis=1)[0:1]
        side_s[k, BASE : BASE + HALO] = corner
        side_s[k, BASE + HALO : BASE + EXT] = left
        side_s[k, BASE + EXT : BASE + EXT + 1] = below
    near_s[0] = pltpu.roll(front_ref[1], 64, axis=1)
    near_s[1] = back_ref[1]

    def derive(i, carry):
        row = pl.multiple_of(i * 8, 8)
        at = pl.multiple_of(row + BASE, 8)
        core = [core_s[k, pl.ds(at, 8)] for k in range(BZ)]
        side = [side_s[k, pl.ds(at, 8)] for k in range(BZ)]
        front = (front_ref[0, pl.ds(row, 8)], near_s[0, pl.ds(row, 8)])
        back = (back_ref[0, pl.ds(row, 8)], near_s[1, pl.ds(row, 8)])
        edge = right_ref[pl.ds(row, 8)]
        for k in range(BZ):
            c, s = core[k], side[k]
            c_next = pltpu.roll(c, TILE - 1, axis=1)
            s_prev = pltpu.roll(s, 1, axis=1)
            c_right = jnp.where(
                lane8 == TILE - 1, pltpu.roll(edge, TILE - 1 - 32 * k, axis=1), c_next
            )
            c_left = jnp.where(lane8 == 0, s_prev, pltpu.roll(c, 1, axis=1))
            s_right = jnp.where(lane8 == TILE - 1, c_next, pltpu.roll(s, TILE - 1, axis=1))
            for half, (value, xr, xl, ref, before, after) in enumerate(
                (
                    (c, c_right, c_left, core_s,
                     front[0] if k == 0 else core[k - 1], back[0] if k == 3 else core[k + 1]),
                    (s, s_right, s_prev, side_s,
                     front[1] if k == 0 else side[k - 1], back[1] if k == 3 else side[k + 1]),
                )
            ):
                gd = 0.5 * (after - before)
                gr = 0.5 * (ref[k, pl.ds(at + 1, 8)] - ref[k, pl.ds(at - 1, 8)])
                gc = 0.5 * (xr - xl)
                factor = lax.rsqrt(gd * gd + gr * gr + gc * gc + 1.0)
                fields[0, k, half, pl.ds(row, 8)] = jnp.tanh(value)
                fields[1, k, half, pl.ds(row, 8)] = gd * factor
                fields[2, k, half, pl.ds(row, 8)] = gr * factor
                fields[3, k, half, pl.ds(row, 8)] = gc * factor
                for c3 in range(3):
                    arg = palette_ref[c3, 0] + palette_ref[c3, 1] * value
                    fields[4 + c3, k, half, pl.ds(row, 8)] = 0.5 + 0.5 * jnp.tanh(0.5 * arg)
        return carry

    lax.fori_loop(0, EXT // 8, derive, 0)

    lane = lax.broadcasted_iota(jnp.int32, (CHUNK, TILE), 1)
    rows = lax.broadcasted_iota(jnp.int32, (CHUNK, TILE), 0)
    for view in range(VIEWS):
        ld = jnp.full((8, TILE), light_ref[view, 0], jnp.float32)
        lr = jnp.full((8, TILE), light_ref[view, 1], jnp.float32)
        lc = jnp.full((8, TILE), light_ref[view, 2], jnp.float32)
        length = jnp.sqrt(ld * ld + lr * lr + lc * lc + 1.0)
        td, tr, tc = ((v / length)[0:1] for v in (ld, lr, lc))
        rate = rate_ref[view]
        off_r, off_c = moves_ref[view * 10 + 8], moves_ref[view * 10 + 9]

        def shade_rows(j, carry, view=view, td=td, tr=tr, tc=tc, rate=rate, off_r=off_r, off_c=off_c):
            base = pl.multiple_of(j * CHUNK, CHUNK)
            inside = jnp.logical_and(
                rows + (gy * TILE + base) >= off_r, lane + gx * TILE >= off_c
            )
            depth = jnp.zeros((CHUNK, TILE), jnp.float32)
            clear = jnp.ones((CHUNK, TILE), jnp.float32)
            color = [jnp.zeros((CHUNK, TILE), jnp.float32) for _ in range(3)]
            for k in range(BZ):
                dy = moves_ref[view * 10 + 2 * k]
                dx = moves_ref[view * 10 + 2 * k + 1]
                start = base + (HALO - dy)
                own = lane < TILE - dx

                def sample(a):
                    core = fields[a, k, 0, pl.ds(start, CHUNK)]
                    side = fields[a, k, 1, pl.ds(start, CHUNK)]
                    return pltpu.roll(jnp.where(own, core, side), dx, axis=1)

                density = rate * (1.0 + sample(0))
                dot = sample(1) * td + sample(2) * tr + sample(3) * tc
                kept = clear * jnp.exp(-density)
                weight = (0.25 + 0.75 * dot * dot) * (clear - kept)
                for c3 in range(3):
                    color[c3] = color[c3] + sample(4 + c3) * weight
                depth = depth + density
                clear = kept
            for c4, value in enumerate(color + [depth]):
                value = jnp.where(inside, value, 0.0)
                for q in range(CHUNK // 4):
                    out_ref[j * (CHUNK // 4) + q, c4 * 16 + view * 4 : c4 * 16 + view * 4 + 4] = (
                        value[4 * q : 4 * q + 4]
                    )
            return carry

        lax.fori_loop(0, TILE // CHUNK, shade_rows, 0)


def composite_kernel(order_ref, pieces_ref, out_ref):
    bricks = pieces_ref.shape[0]
    for view in range(VIEWS):
        cover = jnp.zeros((4, TILE), jnp.float32)
        color = [jnp.zeros((4, TILE), jnp.float32) for _ in range(3)]
        for place in range(bricks):
            brick = order_ref[view, place]
            clear = jnp.exp(-cover)
            for c3 in range(3):
                at = c3 * 16 + view * 4
                color[c3] = color[c3] + pieces_ref[brick, at : at + 4] * clear
            at = 48 + view * 4
            cover = cover + pieces_ref[brick, at : at + 4]
        for c3 in range(3):
            out_ref[view, c3, 0] = color[c3]
        out_ref[view, 3, 0] = 1.0 - jnp.exp(-cover)


def moved(value, axes, steps):
    count = lax.axis_size(axes)
    first, last = max(0, -steps), min(count, count - steps)
    return lax.ppermute(value, axes, [(i, i + steps) for i in range(first, last)])


def diagonal(value):
    n_y, n_x = lax.axis_size("gy"), lax.axis_size("gx")
    pairs = [
        (y * n_x + x, (y + 1) * n_x + x + 1) for y in range(n_y - 1) for x in range(n_x - 1)
    ]
    return lax.ppermute(value, ("gy", "gx"), pairs)


def on_device(pressure, light, palette, rate, shear, offset, order):
    bricks = order.shape[1]
    brick = lax.axis_index("gz")
    zero = jnp.zeros((), jnp.int32)

    shifts = lax.dynamic_slice(shear, (zero, brick * BZ, zero), (VIEWS, BZ, 2))
    place = lax.dynamic_slice(offset, (zero, brick, zero), (VIEWS, 1, 2))
    moves = jnp.concatenate([shifts + place, place], axis=1).reshape(-1)

    half = TILE // 2
    pack = jnp.concatenate(
        [
            jnp.stack([pressure[3, :, half:], pressure[2, :, half:]]),
            jnp.stack([pressure[0, :, half:], pressure[1, :, half:]]),
        ],
        axis=2,
    )
    above = moved(pressure[:, TILE - HALO :], "gy", 1)
    left = moved(pack, "gx", 1)
    corner = diagonal(pack[:, TILE - HALO :])

    def slice_with_margins(k):
        return jnp.stack(
            [
                jnp.concatenate([above[k], pressure[k]], axis=0),
                jnp.concatenate([corner[0], left[0]], axis=0),
            ]
        )

    front = moved(slice_with_margins(3), "gz", 1)
    back = moved(slice_with_margins(0), "gz", -1)
    below = moved(jnp.concatenate([pressure[:, 0], left[:, 0]], axis=0), "gy", -1)
    edge = jnp.concatenate(
        [jnp.concatenate([above[k, :, :32], pressure[k, :, :32]], axis=0) for k in range(BZ)], axis=1
    )
    right = moved(edge, "gx", -1)

    pieces = pl.pallas_call(
        render_kernel,
        out_shape=jax.ShapeDtypeStruct((bricks, 4 * VIEWS * 4, TILE), jnp.float32),
        in_specs=[SMEM] * 4 + [VMEM] * 8,
        out_specs=VMEM,
        scratch_shapes=[
            pltpu.VMEM((BZ, BASE + EXT + 8, TILE), jnp.float32),
            pltpu.VMEM((BZ, BASE + EXT + 8, TILE), jnp.float32),
            pltpu.VMEM((2, EXT, TILE), jnp.float32),
            pltpu.VMEM((7, BZ, 2, EXT, TILE), jnp.float32),
        ],
        compiler_params=pltpu.CompilerParams(vmem_limit_bytes=32 * 1024 * 1024),
        name="render",
    )(moves, light, palette, rate, pressure, above, left, corner, front, back, below, right)

    strips = lax.all_to_all(pieces, "gz", 0, 0, tiled=True)

    return pl.pallas_call(
        composite_kernel,
        out_shape=jax.ShapeDtypeStruct((VIEWS, 4, 1, 4, TILE), jnp.float32),
        in_specs=[SMEM, VMEM],
        out_specs=VMEM,
        compiler_params=pltpu.CompilerParams(vmem_limit_bytes=16 * 1024 * 1024),
        name="composite",
    )(order, strips)


def solution(mesh):
    return jax.shard_map(
        on_device,
        mesh=mesh,
        in_specs=(P("gz", "gy", "gx"), P(), P(), P(), P(), P(), P()),
        out_specs=P(None, None, "gz", "gy", "gx"),
        check_vma=False,
    )
```

```python
import functools

import jax
import jax.numpy as jnp
from jax import lax
from jax.experimental import pallas as pl
from jax.experimental.pallas import tpu as pltpu
from jax.sharding import PartitionSpec as P

VIEWS = 4
BZ = 4
TILE = 128
HALO = 40
EXT = HALO + TILE
BASE = 8
CHUNK = 16

VMEM = pl.BlockSpec(memory_space=pltpu.VMEM)
SMEM = pl.BlockSpec(memory_space=pltpu.SMEM)


def pack_kernel(own_ref, last_ref, pack_ref):
    lane = lax.broadcasted_iota(jnp.int32, (TILE, TILE), 1)
    last_ref[...] = own_ref[:, TILE - HALO :]
    for k in range(2):
        pack_ref[k] = jnp.where(
            lane < TILE // 2, pltpu.roll(own_ref[3 - k], TILE // 2, axis=1), own_ref[k]
        )


def left_margin(left_ref, k):
    return left_ref[k] if k < 2 else pltpu.roll(left_ref[3 - k], TILE // 2, axis=1)


def render_kernel(
    shear_ref, offset_ref, light_ref, palette_ref, rate_ref,
    own_ref, above_ref, left_ref, corner_ref, front_ref, back_ref, below_ref, right_ref,
    out_ref,
    core_s, side_s, near_s, fields,
):
    brick = lax.axis_index("gz")
    gy = lax.axis_index("gy")
    gx = lax.axis_index("gx")
    lane8 = lax.broadcasted_iota(jnp.int32, (8, TILE), 1)

    for k in range(BZ):
        core_s[k, BASE : BASE + HALO] = above_ref[k]
        core_s[k, BASE + HALO : BASE + EXT] = own_ref[k]
        core_s[k, BASE + EXT : BASE + EXT + 1] = below_ref[k : k + 1]
        side_s[k, BASE : BASE + HALO] = corner_ref[k]
        side_s[k, BASE + HALO : BASE + EXT] = left_margin(left_ref, k)
        row = jnp.broadcast_to(below_ref[BZ + min(k, 3 - k) : BZ + min(k, 3 - k) + 1], (8, TILE))
        if k >= 2:
            row = pltpu.roll(row, TILE // 2, axis=1)
        side_s[k, BASE + EXT : BASE + EXT + 1] = row[:1]
    near_s[:HALO] = front_ref[1, :HALO]
    near_s[HALO:] = pltpu.roll(front_ref[1, HALO:], TILE // 2, axis=1)

    def derive(i, carry):
        row = pl.multiple_of(i * 8, 8)
        at = pl.multiple_of(row + BASE, 8)
        core = [core_s[k, pl.ds(at, 8)] for k in range(BZ)]
        side = [side_s[k, pl.ds(at, 8)] for k in range(BZ)]
        front = (front_ref[0, pl.ds(row, 8)], near_s[pl.ds(row, 8)])
        back = (back_ref[0, pl.ds(row, 8)], back_ref[1, pl.ds(row, 8)])
        edge = right_ref[pl.ds(row, 8)]
        for k in range(BZ):
            c, s = core[k], side[k]
            c_next = pltpu.roll(c, TILE - 1, axis=1)
            s_prev = pltpu.roll(s, 1, axis=1)
            c_right = jnp.where(
                lane8 == TILE - 1, pltpu.roll(edge, TILE - 1 - 32 * k, axis=1), c_next
            )
            c_left = jnp.where(lane8 == 0, s_prev, pltpu.roll(c, 1, axis=1))
            s_right = jnp.where(lane8 == TILE - 1, c_next, pltpu.roll(s, TILE - 1, axis=1))
            for half, (value, xr, xl, ref, before, after) in enumerate(
                (
                    (c, c_right, c_left, core_s,
                     front[0] if k == 0 else core[k - 1], back[0] if k == 3 else core[k + 1]),
                    (s, s_right, s_prev, side_s,
                     front[1] if k == 0 else side[k - 1], back[1] if k == 3 else side[k + 1]),
                )
            ):
                gd = 0.5 * (after - before)
                gr = 0.5 * (ref[k, pl.ds(at + 1, 8)] - ref[k, pl.ds(at - 1, 8)])
                gc = 0.5 * (xr - xl)
                factor = lax.rsqrt(gd * gd + gr * gr + gc * gc + 1.0)
                fields[0, k, half, pl.ds(row, 8)] = jnp.tanh(value)
                fields[1, k, half, pl.ds(row, 8)] = gd * factor
                fields[2, k, half, pl.ds(row, 8)] = gr * factor
                fields[3, k, half, pl.ds(row, 8)] = gc * factor
                for c3 in range(3):
                    arg = palette_ref[0, c3] + palette_ref[1, c3] * value
                    fields[4 + c3, k, half, pl.ds(row, 8)] = 0.5 + 0.5 * jnp.tanh(0.5 * arg)
        return carry

    lax.fori_loop(0, EXT // 8, derive, 0, unroll=3)

    lane = lax.broadcasted_iota(jnp.int32, (CHUNK, TILE), 1)
    rows = lax.broadcasted_iota(jnp.int32, (CHUNK, TILE), 0)
    for view in range(VIEWS):
        ld = jnp.full((8, TILE), light_ref[view, 0], jnp.float32)
        lr = jnp.full((8, TILE), light_ref[view, 1], jnp.float32)
        lc = jnp.full((8, TILE), light_ref[view, 2], jnp.float32)
        length = jnp.sqrt(ld * ld + lr * lr + lc * lc + 1.0)
        td, tr, tc = ((v / length)[0:1] for v in (ld, lr, lc))
        rate = rate_ref[view]
        off_r, off_c = offset_ref[view, 0, brick], offset_ref[view, 1, brick]

        def shade_rows(j, carry, view=view, td=td, tr=tr, tc=tc, rate=rate, off_r=off_r, off_c=off_c):
            base = pl.multiple_of(j * CHUNK, CHUNK)
            inside = jnp.logical_and(
                rows + (gy * TILE + base) >= off_r, lane + gx * TILE >= off_c
            )
            depth = jnp.zeros((CHUNK, TILE), jnp.float32)
            clear = jnp.ones((CHUNK, TILE), jnp.float32)
            color = [jnp.zeros((CHUNK, TILE), jnp.float32) for _ in range(3)]
            for k in range(BZ):
                dy = off_r + shear_ref[view, 0, brick * BZ + k]
                dx = off_c + shear_ref[view, 1, brick * BZ + k]
                start = base + (HALO - dy)
                own = lane < TILE - dx

                def sample(a):
                    core = fields[a, k, 0, pl.ds(start, CHUNK)]
                    side = fields[a, k, 1, pl.ds(start, CHUNK)]
                    return pltpu.roll(jnp.where(own, core, side), dx, axis=1)

                density = rate * (1.0 + sample(0))
                dot = sample(1) * td + sample(2) * tr + sample(3) * tc
                kept = clear * jnp.exp(-density)
                weight = (0.25 + 0.75 * dot * dot) * (clear - kept)
                for c3 in range(3):
                    color[c3] = color[c3] + sample(4 + c3) * weight
                depth = depth + density
                clear = kept
            for c4, value in enumerate(color + [depth]):
                value = jnp.where(inside, value, 0.0)
                for q in range(CHUNK // 4):
                    out_ref[j * (CHUNK // 4) + q, c4 * 16 + view * 4 : c4 * 16 + view * 4 + 4] = (
                        value[4 * q : 4 * q + 4]
                    )
            return carry

        lax.fori_loop(0, TILE // CHUNK, shade_rows, 0, unroll=True)


def composite_kernel(order_ref, pieces_ref, out_ref):
    bricks = pieces_ref.shape[0]
    for view in range(VIEWS):
        cover = jnp.zeros((4, TILE), jnp.float32)
        color = [jnp.zeros((4, TILE), jnp.float32) for _ in range(3)]
        for place in range(bricks):
            brick = order_ref[view, place]
            clear = jnp.exp(-cover)
            for c3 in range(3):
                at = c3 * 16 + view * 4
                color[c3] = color[c3] + pieces_ref[brick, at : at + 4] * clear
            at = 48 + view * 4
            cover = cover + pieces_ref[brick, at : at + 4]
        for c3 in range(3):
            out_ref[view, c3, 0] = color[c3]
        out_ref[view, 3, 0] = 1.0 - jnp.exp(-cover)


def moved(value, axes, steps):
    count = lax.axis_size(axes)
    first, last = max(0, -steps), min(count, count - steps)
    return lax.ppermute(value, axes, [(i, i + steps) for i in range(first, last)])


def diagonal(value):
    n_y, n_x = lax.axis_size("gy"), lax.axis_size("gx")
    pairs = [
        (y * n_x + x, (y + 1) * n_x + x + 1) for y in range(n_y - 1) for x in range(n_x - 1)
    ]
    return lax.ppermute(value, ("gy", "gx"), pairs)


def on_device(pressure, light, palette, rate, shear, offset, order):
    bricks = order.shape[1]

    def shapes(*dims):
        return [jax.ShapeDtypeStruct(dim, jnp.float32) for dim in dims]

    last, pack = pl.pallas_call(
        pack_kernel,
        out_shape=shapes((BZ, HALO, TILE), (2, TILE, TILE)),
        in_specs=[VMEM],
        out_specs=[VMEM] * 2,
        compiler_params=pltpu.CompilerParams(vmem_limit_bytes=8 * 1024 * 1024),
        name="pack",
    )(pressure)
    above = moved(last, "gy", 1)
    left = moved(pack, "gx", 1)
    corner = diagonal(last)

    def slice_with_margins(k, margin):
        return jnp.stack(
            [
                jnp.concatenate([above[k], pressure[k]], axis=0),
                jnp.concatenate([corner[k], margin], axis=0),
            ]
        )

    front = moved(slice_with_margins(3, left[0]), "gz", 1)
    back = moved(slice_with_margins(0, left[0]), "gz", -1)
    below = moved(jnp.concatenate([pressure[:, 0], left[:, 0]], axis=0), "gy", -1)
    edge = jnp.concatenate(
        [jnp.concatenate([above[k, :, :32], pressure[k, :, :32]], axis=0) for k in range(BZ)], axis=1
    )
    right = moved(edge, "gx", -1)

    pieces = pl.pallas_call(
        render_kernel,
        out_shape=jax.ShapeDtypeStruct((bricks, 4 * VIEWS * 4, TILE), jnp.float32),
        in_specs=[SMEM] * 5 + [VMEM] * 8,
        out_specs=VMEM,
        scratch_shapes=[
            pltpu.VMEM((BZ, BASE + EXT + 8, TILE), jnp.float32),
            pltpu.VMEM((BZ, BASE + EXT + 8, TILE), jnp.float32),
            pltpu.VMEM((EXT, TILE), jnp.float32),
            pltpu.VMEM((7, BZ, 2, EXT, TILE), jnp.float32),
        ],
        compiler_params=pltpu.CompilerParams(vmem_limit_bytes=32 * 1024 * 1024),
        name="render",
    )(
        shear.transpose(0, 2, 1), offset.transpose(0, 2, 1), light, palette.T, rate, pressure, above, left,
        corner, front, back, below, right,
    )

    strips = lax.all_to_all(pieces, "gz", 0, 0, tiled=True)

    return pl.pallas_call(
        composite_kernel,
        out_shape=jax.ShapeDtypeStruct((VIEWS, 4, 1, 4, TILE), jnp.float32),
        in_specs=[SMEM, VMEM],
        out_specs=VMEM,
        compiler_params=pltpu.CompilerParams(vmem_limit_bytes=16 * 1024 * 1024),
        name="composite",
    )(order, strips)


def solution(mesh):
    return jax.shard_map(
        on_device,
        mesh=mesh,
        in_specs=(P("gz", "gy", "gx"), P(), P(), P(), P(), P(), P()),
        out_specs=P(None, None, "gz", "gy", "gx"),
        check_vma=False,
    )
```

```python
import jax
import jax.numpy as jnp
from jax import lax
from jax.experimental import pallas as pl
from jax.experimental.pallas import tpu as pltpu
from jax.sharding import PartitionSpec as P

VIEWS = 4
BZ = 4
TILE = 128
HALO = 40
EXT = HALO + TILE
CHUNK = 16

VMEM = pl.BlockSpec(memory_space=pltpu.VMEM)
SMEM = pl.BlockSpec(memory_space=pltpu.SMEM)
MEDIUM = pltpu.CompilerParams(vmem_limit_bytes=20 * 1024 * 1024)
SMALL = pltpu.CompilerParams(vmem_limit_bytes=8 * 1024 * 1024)


def pack_kernel(own_ref, last_ref, pack_ref, copy_ref):
    lane = lax.broadcasted_iota(jnp.int32, (TILE, TILE), 1)
    last_ref[...] = own_ref[:, TILE - HALO :]
    copy_ref[...] = own_ref[...]
    for k in range(2):
        pack_ref[k] = jnp.where(
            lane < TILE // 2, pltpu.roll(own_ref[3 - k], TILE // 2, axis=1), own_ref[k]
        )


def left_margin(left_ref, k):
    return left_ref[k] if k < 2 else pltpu.roll(left_ref[3 - k], TILE // 2, axis=1)


def inside_image(base, off_r, off_c):
    shape = (CHUNK, TILE)
    rows = lax.broadcasted_iota(jnp.int32, shape, 0) + (lax.axis_index("gy") * TILE + base)
    cols = lax.broadcasted_iota(jnp.int32, shape, 1) + lax.axis_index("gx") * TILE
    return jnp.logical_and(rows >= off_r, cols >= off_c)


def sampler(shear_ref, offset_ref, view, k, base):
    brick = lax.axis_index("gz")
    dy = offset_ref[view, 0, brick] + shear_ref[view, 0, brick * BZ + k]
    dx = offset_ref[view, 1, brick] + shear_ref[view, 1, brick * BZ + k]
    rows = pl.ds(base + (HALO - dy), CHUNK)
    own = lax.broadcasted_iota(jnp.int32, (CHUNK, TILE), 1) < TILE - dx

    def sample(ref, a):
        return pltpu.roll(jnp.where(own, ref[a, k, 0, rows], ref[a, k, 1, rows]), dx, axis=1)

    return sample


def store_strips(pieces_ref, base, row, value):
    for q in range(CHUNK // 4):
        pieces_ref[base // 4 + q, row : row + 4] = value[4 * q : 4 * q + 4]


def tone_kernel(
    shear_ref, offset_ref, palette_ref, rate_ref, own_ref, above_ref, left_ref, corner_ref,
    pieces_ref, tones_ref, cells_ref,
    fields,
):
    def tone(value, k, half, rows):
        cells_ref[k, half, rows] = value
        fields[0, k, half, rows] = jnp.tanh(value)
        for c3 in range(3):
            arg = palette_ref[0, c3] + palette_ref[1, c3] * value
            fields[1 + c3, k, half, rows] = 0.5 + 0.5 * jnp.tanh(0.5 * arg)

    for k in range(BZ):
        tone(above_ref[k], k, 0, slice(0, HALO))
        tone(own_ref[k], k, 0, slice(HALO, EXT))
        tone(corner_ref[k], k, 1, slice(0, HALO))
        tone(left_margin(left_ref, k), k, 1, slice(HALO, EXT))

    brick = lax.axis_index("gz")
    for view in range(VIEWS):
        off_r, off_c = offset_ref[view, 0, brick], offset_ref[view, 1, brick]
        rate = rate_ref[view]
        for base in range(0, TILE, CHUNK):
            depth = jnp.zeros((CHUNK, TILE), jnp.float32)
            clear = inside_image(base, off_r, off_c).astype(jnp.float32)
            inside = clear
            for k in range(BZ):
                sample = sampler(shear_ref, offset_ref, view, k, base)
                density = rate * (1.0 + sample(fields, 0))
                kept = clear * jnp.exp(-density)
                weight = clear - kept
                for c3 in range(3):
                    tones_ref[view, k, c3, base : base + CHUNK] = sample(fields, 1 + c3) * weight
                depth = depth + density
                clear = kept
            store_strips(pieces_ref, base, 48 + view * 4, depth * inside)


def render_kernel(
    shear_ref, offset_ref, light_ref,
    _, tones_ref, cells_ref, front_ref, back_ref, below_ref, right_ref,
    pieces_ref,
    normals,
):
    lane8 = lax.broadcasted_iota(jnp.int32, (8, TILE), 1)
    row8 = lax.broadcasted_iota(jnp.int32, (8, TILE), 0)

    for i in range(EXT // 8):
        row = slice(8 * i, 8 * i + 8)
        cells = [[cells_ref[k, half, row] for half in range(2)] for k in range(BZ)]
        front = [front_ref[0, row], front_ref[1, row]]
        if 8 * i >= HALO:
            front[1] = pltpu.roll(front[1], TILE // 2, axis=1)
        back = [back_ref[0, row], back_ref[1, row]]
        edge = right_ref[row]
        for k in range(BZ):
            c, s = cells[k]
            c_next = pltpu.roll(c, TILE - 1, axis=1)
            s_prev = pltpu.roll(s, 1, axis=1)
            c_right = jnp.where(
                lane8 == TILE - 1, pltpu.roll(edge, TILE - 1 - 32 * k, axis=1), c_next
            )
            c_left = jnp.where(lane8 == 0, s_prev, pltpu.roll(c, 1, axis=1))
            s_right = jnp.where(lane8 == TILE - 1, c_next, pltpu.roll(s, TILE - 1, axis=1))
            before = front if k == 0 else cells[k - 1]
            after = back if k == BZ - 1 else cells[k + 1]
            for half, (right, left) in enumerate(((c_right, c_left), (s_right, s_prev))):
                if i == 0:
                    upper = pltpu.roll(cells[k][half], 1, axis=0)
                else:
                    upper = cells_ref[k, half, 8 * i - 1 : 8 * i + 7]
                if i < EXT // 8 - 1:
                    lower = cells_ref[k, half, 8 * i + 1 : 8 * i + 9]
                else:
                    at = k if half == 0 else BZ + min(k, 3 - k)
                    last = jnp.broadcast_to(below_ref[at : at + 1], (8, TILE))
                    if half == 1 and k >= 2:
                        last = pltpu.roll(last, TILE // 2, axis=1)
                    lower = jnp.where(row8 == 7, last, pltpu.roll(cells[k][half], 7, axis=0))
                gd = 0.5 * (after[half] - before[half])
                gr = 0.5 * (lower - upper)
                gc = 0.5 * (right - left)
                factor = lax.rsqrt(gd * gd + gr * gr + gc * gc + 1.0)
                normals[0, k, half, row] = gd * factor
                normals[1, k, half, row] = gr * factor
                normals[2, k, half, row] = gc * factor

    for view in range(VIEWS):
        ld = jnp.full((8, TILE), light_ref[view, 0], jnp.float32)
        lr = jnp.full((8, TILE), light_ref[view, 1], jnp.float32)
        lc = jnp.full((8, TILE), light_ref[view, 2], jnp.float32)
        length = jnp.sqrt(ld * ld + lr * lr + lc * lc + 1.0)
        td, tr, tc = ((v / length)[0:1] for v in (ld, lr, lc))
        for base in range(0, TILE, CHUNK):
            color = [jnp.zeros((CHUNK, TILE), jnp.float32) for _ in range(3)]
            for k in range(BZ):
                sample = sampler(shear_ref, offset_ref, view, k, base)
                dot = sample(normals, 0) * td + sample(normals, 1) * tr + sample(normals, 2) * tc
                shade = 0.25 + 0.75 * dot * dot
                for c3 in range(3):
                    color[c3] = color[c3] + tones_ref[view, k, c3, base : base + CHUNK] * shade
            for c3 in range(3):
                store_strips(pieces_ref, base, c3 * 16 + view * 4, color[c3])


def composite_kernel(order_ref, pieces_ref, out_ref):
    bricks = pieces_ref.shape[0]
    for view in range(VIEWS):
        cover = jnp.zeros((4, TILE), jnp.float32)
        color = [jnp.zeros((4, TILE), jnp.float32) for _ in range(3)]
        for place in range(bricks):
            brick = order_ref[view, place]
            clear = jnp.exp(-cover)
            for c3 in range(3):
                at = c3 * 16 + view * 4
                color[c3] = color[c3] + pieces_ref[brick, at : at + 4] * clear
            at = 48 + view * 4
            cover = cover + pieces_ref[brick, at : at + 4]
        for c3 in range(3):
            out_ref[view, c3, 0] = color[c3]
        out_ref[view, 3, 0] = 1.0 - jnp.exp(-cover)


def moved(value, axes, steps):
    count = lax.axis_size(axes)
    first, last = max(0, -steps), min(count, count - steps)
    return lax.ppermute(value, axes, [(i, i + steps) for i in range(first, last)])


def diagonal(value):
    n_y, n_x = lax.axis_size("gy"), lax.axis_size("gx")
    pairs = [
        (y * n_x + x, (y + 1) * n_x + x + 1) for y in range(n_y - 1) for x in range(n_x - 1)
    ]
    return lax.ppermute(value, ("gy", "gx"), pairs)


def on_device(pressure, light, palette, rate, shear, offset, order):
    bricks = order.shape[1]

    def shapes(*dims):
        return [jax.ShapeDtypeStruct(dim, jnp.float32) for dim in dims]

    last, pack, own = pl.pallas_call(
        pack_kernel,
        out_shape=shapes((BZ, HALO, TILE), (2, TILE, TILE), (BZ, TILE, TILE)),
        in_specs=[VMEM],
        out_specs=[VMEM] * 3,
        compiler_params=SMALL,
        name="pack",
    )(pressure)
    above = moved(last, "gy", 1)
    left = moved(pack, "gx", 1)
    corner = diagonal(last)

    def slice_with_margins(k, margin):
        return jnp.stack(
            [
                jnp.concatenate([above[k], own[k]], axis=0),
                jnp.concatenate([corner[k], margin], axis=0),
            ]
        )

    front = moved(slice_with_margins(3, left[0]), "gz", 1)
    back = moved(slice_with_margins(0, left[0]), "gz", -1)
    below = moved(jnp.concatenate([own[:, 0], left[:, 0]], axis=0), "gy", -1)
    edge = jnp.concatenate(
        [jnp.concatenate([above[k, :, :32], own[k, :, :32]], axis=0) for k in range(BZ)], axis=1
    )
    right = moved(edge, "gx", -1)

    shears, offsets = shear.transpose(0, 2, 1), offset.transpose(0, 2, 1)
    strips_shape = (bricks, 4 * VIEWS * 4, TILE)
    pieces, tones, cells = pl.pallas_call(
        tone_kernel,
        out_shape=shapes(strips_shape, (VIEWS, BZ, 3, TILE, TILE), (BZ, 2, EXT, TILE)),
        in_specs=[SMEM] * 4 + [VMEM] * 4,
        out_specs=[VMEM] * 3,
        scratch_shapes=[pltpu.VMEM((4, BZ, 2, EXT, TILE), jnp.float32)],
        compiler_params=MEDIUM,
        cost_estimate=pl.CostEstimate(
            flops=10**7, bytes_accessed=4 * 10**6, transcendentals=3 * 10**6
        ),
        name="tone",
    )(shears, offsets, palette.T, rate, own, above, left, corner)
    (pieces,) = pl.pallas_call(
        render_kernel,
        out_shape=shapes(strips_shape),
        in_specs=[SMEM] * 3 + [VMEM] * 7,
        out_specs=[VMEM],
        input_output_aliases={3: 0},
        scratch_shapes=[pltpu.VMEM((3, BZ, 2, EXT, TILE), jnp.float32)],
        compiler_params=MEDIUM,
        name="render",
    )(shears, offsets, light, pieces, tones, cells, front, back, below, right)

    strips = lax.all_to_all(pieces, "gz", 0, 0, tiled=True)

    return pl.pallas_call(
        composite_kernel,
        out_shape=jax.ShapeDtypeStruct((VIEWS, 4, 1, 4, TILE), jnp.float32),
        in_specs=[SMEM, VMEM],
        out_specs=VMEM,
        compiler_params=pltpu.CompilerParams(vmem_limit_bytes=16 * 1024 * 1024),
        name="composite",
    )(order, strips)


def solution(mesh):
    return jax.shard_map(
        on_device,
        mesh=mesh,
        in_specs=(P("gz", "gy", "gx"), P(), P(), P(), P(), P(), P()),
        out_specs=P(None, None, "gz", "gy", "gx"),
        check_vma=False,
    )
```

```python
import jax
import jax.numpy as jnp
from jax import lax
from jax.experimental import pallas as pl
from jax.experimental.pallas import tpu as pltpu
from jax.sharding import PartitionSpec as P

VIEWS = 4
BZ = 4
TILE = 128
HALO = 40
EXT = HALO + TILE
CHUNK = 16

VMEM = pl.BlockSpec(memory_space=pltpu.VMEM)
SMEM = pl.BlockSpec(memory_space=pltpu.SMEM)
MEDIUM = pltpu.CompilerParams(vmem_limit_bytes=20 * 1024 * 1024)
SMALL = pltpu.CompilerParams(vmem_limit_bytes=8 * 1024 * 1024)


def pack_kernel(own_ref, last_ref, pack_ref, copy_ref):
    lane = lax.broadcasted_iota(jnp.int32, (TILE, TILE), 1)
    last_ref[...] = own_ref[:, TILE - HALO :]
    copy_ref[...] = own_ref[...]
    for k in range(2):
        pack_ref[k] = jnp.where(
            lane < TILE // 2, pltpu.roll(own_ref[3 - k], TILE // 2, axis=1), own_ref[k]
        )


def left_margin(left_ref, k):
    return left_ref[k] if k < 2 else pltpu.roll(left_ref[3 - k], TILE // 2, axis=1)


def inside_image(base, off_r, off_c):
    shape = (CHUNK, TILE)
    rows = lax.broadcasted_iota(jnp.int32, shape, 0) + (lax.axis_index("gy") * TILE + base)
    cols = lax.broadcasted_iota(jnp.int32, shape, 1) + lax.axis_index("gx") * TILE
    return jnp.logical_and(rows >= off_r, cols >= off_c)


def sampler(shear_ref, offset_ref, view, k, base):
    brick = lax.axis_index("gz")
    dy = offset_ref[view, 0, brick] + shear_ref[view, 0, brick * BZ + k]
    dx = offset_ref[view, 1, brick] + shear_ref[view, 1, brick * BZ + k]
    rows = pl.ds(base + (HALO - dy), CHUNK)
    own = lax.broadcasted_iota(jnp.int32, (CHUNK, TILE), 1) < TILE - dx

    def sample(ref, a):
        return pltpu.roll(jnp.where(own, ref[a, k, 0, rows], ref[a, k, 1, rows]), dx, axis=1)

    return sample


def store_strips(pieces_ref, base, row, value):
    for q in range(CHUNK // 4):
        pieces_ref[base // 4 + q, row : row + 4] = value[4 * q : 4 * q + 4]


def tone_kernel(
    shear_ref, offset_ref, palette_ref, rate_ref, own_ref, above_ref, left_ref, corner_ref,
    pieces_ref, tones_ref, cells_ref,
    fields,
):
    def tone(value, k, half, rows):
        cells_ref[k, half, rows] = value
        fields[0, k, half, rows] = jnp.tanh(value)
        for c3 in range(3):
            arg = palette_ref[0, c3] + palette_ref[1, c3] * value
            fields[1 + c3, k, half, rows] = 0.5 + 0.5 * jnp.tanh(0.5 * arg)

    for k in range(BZ):
        tone(above_ref[k], k, 0, slice(0, HALO))
        tone(own_ref[k], k, 0, slice(HALO, EXT))
        tone(corner_ref[k], k, 1, slice(0, HALO))
        tone(left_margin(left_ref, k), k, 1, slice(HALO, EXT))

    brick = lax.axis_index("gz")
    for view in range(VIEWS):
        off_r, off_c = offset_ref[view, 0, brick], offset_ref[view, 1, brick]
        rate = rate_ref[view]
        for base in range(0, TILE, CHUNK):
            depth = jnp.zeros((CHUNK, TILE), jnp.float32)
            clear = inside_image(base, off_r, off_c).astype(jnp.float32)
            inside = clear
            for k in range(BZ):
                sample = sampler(shear_ref, offset_ref, view, k, base)
                density = rate * (1.0 + sample(fields, 0))
                kept = clear * jnp.exp(-density)
                weight = clear - kept
                for c3 in range(3):
                    tones_ref[view, k, c3, base : base + CHUNK] = sample(fields, 1 + c3) * weight
                depth = depth + density
                clear = kept
            store_strips(pieces_ref, base, 48 + view * 4, depth * inside)


def render_kernel(
    shear_ref, offset_ref, light_ref,
    _, tones_ref, cells_ref, inner_ref, outer_ref, below_ref, right_ref,
    pieces_ref,
    normals,
):
    lane8 = lax.broadcasted_iota(jnp.int32, (8, TILE), 1)
    row8 = lax.broadcasted_iota(jnp.int32, (8, TILE), 0)
    even = jnp.full((8, TILE), lax.axis_index("gz"), jnp.int32) % 2 == 0

    for i in range(EXT // 8):
        row = slice(8 * i, 8 * i + 8)
        cells = [[cells_ref[k, half, row] for half in range(2)] for k in range(BZ)]
        inner = [inner_ref[half, row] for half in range(2)]
        outer = [outer_ref[half, row] for half in range(2)]
        front = [jnp.where(even, b, a) for b, a in zip(outer, inner, strict=True)]
        back = [jnp.where(even, a, b) for b, a in zip(outer, inner, strict=True)]
        if 8 * i >= HALO:
            front[1] = pltpu.roll(front[1], TILE // 2, axis=1)
        edge = right_ref[row]
        for k in range(BZ):
            c, s = cells[k]
            c_next = pltpu.roll(c, TILE - 1, axis=1)
            s_prev = pltpu.roll(s, 1, axis=1)
            c_right = jnp.where(
                lane8 == TILE - 1, pltpu.roll(edge, TILE - 1 - 32 * k, axis=1), c_next
            )
            c_left = jnp.where(lane8 == 0, s_prev, pltpu.roll(c, 1, axis=1))
            s_right = jnp.where(lane8 == TILE - 1, c_next, pltpu.roll(s, TILE - 1, axis=1))
            before = front if k == 0 else cells[k - 1]
            after = back if k == BZ - 1 else cells[k + 1]
            for half, (right, left) in enumerate(((c_right, c_left), (s_right, s_prev))):
                if i == 0:
                    upper = pltpu.roll(cells[k][half], 1, axis=0)
                else:
                    upper = cells_ref[k, half, 8 * i - 1 : 8 * i + 7]
                if i < EXT // 8 - 1:
                    lower = cells_ref[k, half, 8 * i + 1 : 8 * i + 9]
                else:
                    at = k if half == 0 else BZ + min(k, 3 - k)
                    last = jnp.broadcast_to(below_ref[at : at + 1], (8, TILE))
                    if half == 1 and k >= 2:
                        last = pltpu.roll(last, TILE // 2, axis=1)
                    lower = jnp.where(row8 == 7, last, pltpu.roll(cells[k][half], 7, axis=0))
                gd = 0.5 * (after[half] - before[half])
                gr = 0.5 * (lower - upper)
                gc = 0.5 * (right - left)
                factor = lax.rsqrt(gd * gd + gr * gr + gc * gc + 1.0)
                normals[0, k, half, row] = gd * factor
                normals[1, k, half, row] = gr * factor
                normals[2, k, half, row] = gc * factor

    for view in range(VIEWS):
        ld = jnp.full((8, TILE), light_ref[view, 0], jnp.float32)
        lr = jnp.full((8, TILE), light_ref[view, 1], jnp.float32)
        lc = jnp.full((8, TILE), light_ref[view, 2], jnp.float32)
        length = jnp.sqrt(ld * ld + lr * lr + lc * lc + 1.0)
        td, tr, tc = ((v / length)[0:1] for v in (ld, lr, lc))
        for base in range(0, TILE, CHUNK):
            color = [jnp.zeros((CHUNK, TILE), jnp.float32) for _ in range(3)]
            for k in range(BZ):
                sample = sampler(shear_ref, offset_ref, view, k, base)
                dot = sample(normals, 0) * td + sample(normals, 1) * tr + sample(normals, 2) * tc
                shade = 0.25 + 0.75 * dot * dot
                for c3 in range(3):
                    color[c3] = color[c3] + tones_ref[view, k, c3, base : base + CHUNK] * shade
            for c3 in range(3):
                store_strips(pieces_ref, base, c3 * 16 + view * 4, color[c3])


def composite_kernel(order_ref, pieces_ref, out_ref):
    bricks = pieces_ref.shape[0]
    for view in range(VIEWS):
        cover = jnp.zeros((4, TILE), jnp.float32)
        color = [jnp.zeros((4, TILE), jnp.float32) for _ in range(3)]
        for place in range(bricks):
            brick = order_ref[view, place]
            clear = jnp.exp(-cover)
            for c3 in range(3):
                at = c3 * 16 + view * 4
                color[c3] = color[c3] + pieces_ref[brick, at : at + 4] * clear
            at = 48 + view * 4
            cover = cover + pieces_ref[brick, at : at + 4]
        for c3 in range(3):
            out_ref[view, c3, 0] = color[c3]
        out_ref[view, 3, 0] = 1.0 - jnp.exp(-cover)


def moved(value, axes, steps):
    count = lax.axis_size(axes)
    first, last = max(0, -steps), min(count, count - steps)
    return lax.ppermute(value, axes, [(i, i + steps) for i in range(first, last)])


def swapped(value, axis, first):
    lows = range(first, lax.axis_size(axis) - 1, 2)
    return lax.ppermute(value, axis, [p for i in lows for p in ((i, i + 1), (i + 1, i))])


def diagonal(value):
    n_y, n_x = lax.axis_size("gy"), lax.axis_size("gx")
    pairs = [
        (y * n_x + x, (y + 1) * n_x + x + 1) for y in range(n_y - 1) for x in range(n_x - 1)
    ]
    return lax.ppermute(value, ("gy", "gx"), pairs)


def on_device(pressure, light, palette, rate, shear, offset, order):
    bricks = order.shape[1]

    def shapes(*dims):
        return [jax.ShapeDtypeStruct(dim, jnp.float32) for dim in dims]

    last, pack, own = pl.pallas_call(
        pack_kernel,
        out_shape=shapes((BZ, HALO, TILE), (2, TILE, TILE), (BZ, TILE, TILE)),
        in_specs=[VMEM],
        out_specs=[VMEM] * 3,
        compiler_params=SMALL,
        name="pack",
    )(pressure)
    above = moved(last, "gy", 1)
    left = moved(pack, "gx", 1)
    corner = diagonal(last)

    def slice_with_margins(k, margin):
        return jnp.stack(
            [
                jnp.concatenate([above[k], own[k]], axis=0),
                jnp.concatenate([corner[k], margin], axis=0),
            ]
        )

    even = lax.axis_index("gz") % 2 == 0
    first, final = slice_with_margins(0, left[0]), slice_with_margins(3, left[0])
    inner = swapped(jnp.where(even, final, first), "gz", 0)
    outer = swapped(jnp.where(even, first, final), "gz", 1)
    below = moved(jnp.concatenate([own[:, 0], left[:, 0]], axis=0), "gy", -1)
    edge = jnp.concatenate(
        [jnp.concatenate([above[k, :, :32], own[k, :, :32]], axis=0) for k in range(BZ)], axis=1
    )
    right = moved(edge, "gx", -1)

    shears, offsets = shear.transpose(0, 2, 1), offset.transpose(0, 2, 1)
    strips_shape = (bricks, 4 * VIEWS * 4, TILE)
    pieces, tones, cells = pl.pallas_call(
        tone_kernel,
        out_shape=shapes(strips_shape, (VIEWS, BZ, 3, TILE, TILE), (BZ, 2, EXT, TILE)),
        in_specs=[SMEM] * 4 + [VMEM] * 4,
        out_specs=[VMEM] * 3,
        scratch_shapes=[pltpu.VMEM((4, BZ, 2, EXT, TILE), jnp.float32)],
        compiler_params=MEDIUM,
        cost_estimate=pl.CostEstimate(
            flops=10**7, bytes_accessed=4 * 10**6, transcendentals=3 * 10**6
        ),
        name="tone",
    )(shears, offsets, palette.T, rate, own, above, left, corner)
    (pieces,) = pl.pallas_call(
        render_kernel,
        out_shape=shapes(strips_shape),
        in_specs=[SMEM] * 3 + [VMEM] * 7,
        out_specs=[VMEM],
        input_output_aliases={3: 0},
        scratch_shapes=[pltpu.VMEM((3, BZ, 2, EXT, TILE), jnp.float32)],
        compiler_params=MEDIUM,
        name="render",
    )(shears, offsets, light, pieces, tones, cells, inner, outer, below, right)

    strips = lax.all_to_all(pieces, "gz", 0, 0, tiled=True)

    return pl.pallas_call(
        composite_kernel,
        out_shape=jax.ShapeDtypeStruct((VIEWS, 4, 1, 4, TILE), jnp.float32),
        in_specs=[SMEM, VMEM],
        out_specs=VMEM,
        compiler_params=pltpu.CompilerParams(vmem_limit_bytes=16 * 1024 * 1024),
        name="composite",
    )(order, strips)


def solution(mesh):
    return jax.shard_map(
        on_device,
        mesh=mesh,
        in_specs=(P("gz", "gy", "gx"), P(), P(), P(), P(), P(), P()),
        out_specs=P(None, None, "gz", "gy", "gx"),
        check_vma=False,
    )
```

```python
import jax
import jax.numpy as jnp
from jax import lax
from jax.experimental import pallas as pl
from jax.experimental.pallas import tpu as pltpu
from jax.sharding import PartitionSpec as P

VIEWS = 4
BZ = 4
TILE = 128
HALO = 40
EXT = HALO + TILE
CHUNK = 16

VMEM = pl.BlockSpec(memory_space=pltpu.VMEM)
MEDIUM = pltpu.CompilerParams(vmem_limit_bytes=20 * 1024 * 1024)
SMALL = pltpu.CompilerParams(vmem_limit_bytes=8 * 1024 * 1024)


def pack_kernel(own_ref, last_ref, pack_ref, copy_ref):
    lane = lax.broadcasted_iota(jnp.int32, (TILE, TILE), 1)
    last_ref[...] = own_ref[:, TILE - HALO :]
    copy_ref[...] = own_ref[...]
    for k in range(2):
        pack_ref[k] = jnp.where(
            lane < TILE // 2, pltpu.roll(own_ref[3 - k], TILE // 2, axis=1), own_ref[k]
        )


def left_margin(left_ref, k):
    return left_ref[k] if k < 2 else pltpu.roll(left_ref[3 - k], TILE // 2, axis=1)


def inside_image(base, off_r, off_c):
    shape = (CHUNK, TILE)
    rows = lax.broadcasted_iota(jnp.int32, shape, 0) + (lax.axis_index("gy") * TILE + base)
    cols = lax.broadcasted_iota(jnp.int32, shape, 1) + lax.axis_index("gx") * TILE
    return jnp.logical_and(rows >= off_r, cols >= off_c)


def moves_of(shear_ref, offset_ref):
    brick = lax.axis_index("gz")
    shear = pltpu.roll(shear_ref[...], shear_ref.shape[2] - brick * BZ, axis=2)
    offset = offset_ref[...]
    here = lax.broadcasted_iota(jnp.int32, offset.shape, 2) == brick
    place = jnp.sum(jnp.where(here, offset, 0), axis=2, keepdims=True)
    total = shear + place
    cells = [[(total[v, 0, k], total[v, 1, k]) for k in range(BZ)] for v in range(VIEWS)]
    return cells, [(place[v, 0, 0], place[v, 1, 0]) for v in range(VIEWS)]


def sampler(move, k, base):
    dy, dx = move
    rows = pl.ds(base + (HALO - dy), CHUNK)
    own = lax.broadcasted_iota(jnp.int32, (CHUNK, TILE), 1) < TILE - dx

    def sample(ref, a):
        return pltpu.roll(jnp.where(own, ref[a, k, 0, rows], ref[a, k, 1, rows]), dx, axis=1)

    return sample


def store_strips(pieces_ref, base, row, value):
    for q in range(CHUNK // 4):
        pieces_ref[base // 4 + q, row : row + 4] = value[4 * q : 4 * q + 4]


def tone_kernel(
    shear_ref, offset_ref, palette_ref, rate_ref, own_ref, above_ref, left_ref, corner_ref,
    pieces_ref, tones_ref, cells_ref,
    fields,
):
    def tone(value, k, half, rows):
        cells_ref[k, half, rows] = value
        fields[0, k, half, rows] = jnp.tanh(value)
        for c3 in range(3):
            arg = palette_ref[0, c3] + palette_ref[1, c3] * value
            fields[1 + c3, k, half, rows] = 0.5 + 0.5 * jnp.tanh(0.5 * arg)

    for k in range(BZ):
        tone(above_ref[k], k, 0, slice(0, HALO))
        tone(own_ref[k], k, 0, slice(HALO, EXT))
        tone(corner_ref[k], k, 1, slice(0, HALO))
        tone(left_margin(left_ref, k), k, 1, slice(HALO, EXT))

    moves, places = moves_of(shear_ref, offset_ref)
    for view in range(VIEWS):
        off_r, off_c = places[view]
        rate = rate_ref[0, view]
        for base in range(0, TILE, CHUNK):
            depth = jnp.zeros((CHUNK, TILE), jnp.float32)
            clear = inside_image(base, off_r, off_c).astype(jnp.float32)
            inside = clear
            for k in range(BZ):
                sample = sampler(moves[view][k], k, base)
                density = rate * (1.0 + sample(fields, 0))
                kept = clear * jnp.exp(-density)
                weight = clear - kept
                for c3 in range(3):
                    tones_ref[view, k, c3, base : base + CHUNK] = sample(fields, 1 + c3) * weight
                depth = depth + density
                clear = kept
            store_strips(pieces_ref, base, 48 + view * 4, depth * inside)


def render_kernel(
    shear_ref, offset_ref, light_ref,
    started_ref, tones_ref, cells_ref, inner_ref, outer_ref, below_ref, right_ref,
    pieces_ref,
    normals,
):
    lane8 = lax.broadcasted_iota(jnp.int32, (8, TILE), 1)
    row8 = lax.broadcasted_iota(jnp.int32, (8, TILE), 0)
    even = jnp.full((8, TILE), lax.axis_index("gz"), jnp.int32) % 2 == 0

    for i in range(EXT // 8):
        row = slice(8 * i, 8 * i + 8)
        cells = [[cells_ref[k, half, row] for half in range(2)] for k in range(BZ)]
        inner = [inner_ref[half, row] for half in range(2)]
        outer = [outer_ref[half, row] for half in range(2)]
        front = [jnp.where(even, b, a) for b, a in zip(outer, inner, strict=True)]
        back = [jnp.where(even, a, b) for b, a in zip(outer, inner, strict=True)]
        if 8 * i >= HALO:
            front[1] = pltpu.roll(front[1], TILE // 2, axis=1)
        edge = right_ref[row]
        for k in range(BZ):
            c, s = cells[k]
            c_next = pltpu.roll(c, TILE - 1, axis=1)
            s_prev = pltpu.roll(s, 1, axis=1)
            c_right = jnp.where(
                lane8 == TILE - 1, pltpu.roll(edge, TILE - 1 - 32 * k, axis=1), c_next
            )
            c_left = jnp.where(lane8 == 0, s_prev, pltpu.roll(c, 1, axis=1))
            s_right = jnp.where(lane8 == TILE - 1, c_next, pltpu.roll(s, TILE - 1, axis=1))
            before = front if k == 0 else cells[k - 1]
            after = back if k == BZ - 1 else cells[k + 1]
            for half, (right, left) in enumerate(((c_right, c_left), (s_right, s_prev))):
                if i == 0:
                    upper = pltpu.roll(cells[k][half], 1, axis=0)
                else:
                    upper = cells_ref[k, half, 8 * i - 1 : 8 * i + 7]
                if i < EXT // 8 - 1:
                    lower = cells_ref[k, half, 8 * i + 1 : 8 * i + 9]
                else:
                    at = k if half == 0 else BZ + min(k, 3 - k)
                    last = jnp.broadcast_to(below_ref[at : at + 1], (8, TILE))
                    if half == 1 and k >= 2:
                        last = pltpu.roll(last, TILE // 2, axis=1)
                    lower = jnp.where(row8 == 7, last, pltpu.roll(cells[k][half], 7, axis=0))
                gd = 0.5 * (after[half] - before[half])
                gr = 0.5 * (lower - upper)
                gc = 0.5 * (right - left)
                factor = lax.rsqrt(gd * gd + gr * gr + gc * gc + 1.0)
                normals[0, k, half, row] = gd * factor
                normals[1, k, half, row] = gr * factor
                normals[2, k, half, row] = gc * factor

    moves, _ = moves_of(shear_ref, offset_ref)
    for view in range(VIEWS):
        ld = jnp.full((8, TILE), light_ref[view, 0], jnp.float32)
        lr = jnp.full((8, TILE), light_ref[view, 1], jnp.float32)
        lc = jnp.full((8, TILE), light_ref[view, 2], jnp.float32)
        length = jnp.sqrt(ld * ld + lr * lr + lc * lc + 1.0)
        td, tr, tc = ((v / length)[0:1] for v in (ld, lr, lc))
        for base in range(0, TILE, CHUNK):
            color = [jnp.zeros((CHUNK, TILE), jnp.float32) for _ in range(3)]
            for k in range(BZ):
                sample = sampler(moves[view][k], k, base)
                dot = sample(normals, 0) * td + sample(normals, 1) * tr + sample(normals, 2) * tc
                shade = 0.25 + 0.75 * dot * dot
                for c3 in range(3):
                    color[c3] = color[c3] + tones_ref[view, k, c3, base : base + CHUNK] * shade
            for c3 in range(3):
                store_strips(pieces_ref, base, c3 * 16 + view * 4, color[c3])


def composite_kernel(order_ref, pieces_ref, out_ref):
    bricks = pieces_ref.shape[0]
    for view in range(VIEWS):
        cover = jnp.zeros((4, TILE), jnp.float32)
        color = [jnp.zeros((4, TILE), jnp.float32) for _ in range(3)]
        for place in range(bricks):
            brick = order_ref[view, place]
            clear = jnp.exp(-cover)
            for c3 in range(3):
                at = c3 * 16 + view * 4
                color[c3] = color[c3] + pieces_ref[brick, at : at + 4] * clear
            at = 48 + view * 4
            cover = cover + pieces_ref[brick, at : at + 4]
        for c3 in range(3):
            out_ref[view, c3, 0] = color[c3]
        out_ref[view, 3, 0] = 1.0 - jnp.exp(-cover)


def moved(value, axes, steps):
    count = lax.axis_size(axes)
    first, last = max(0, -steps), min(count, count - steps)
    return lax.ppermute(value, axes, [(i, i + steps) for i in range(first, last)])


def swapped(value, axis, first):
    lows = range(first, lax.axis_size(axis) - 1, 2)
    return lax.ppermute(value, axis, [p for i in lows for p in ((i, i + 1), (i + 1, i))])


def diagonal(value):
    n_y, n_x = lax.axis_size("gy"), lax.axis_size("gx")
    pairs = [
        (y * n_x + x, (y + 1) * n_x + x + 1) for y in range(n_y - 1) for x in range(n_x - 1)
    ]
    return lax.ppermute(value, ("gy", "gx"), pairs)


def on_device(pressure, light, palette, rate, shear, offset, order):
    bricks = order.shape[1]

    def shapes(*dims):
        return [jax.ShapeDtypeStruct(dim, jnp.float32) for dim in dims]

    last, pack, own = pl.pallas_call(
        pack_kernel,
        out_shape=shapes((BZ, HALO, TILE), (2, TILE, TILE), (BZ, TILE, TILE)),
        in_specs=[VMEM],
        out_specs=[VMEM] * 3,
        compiler_params=SMALL,
        name="pack",
    )(pressure)
    above = moved(last, "gy", 1)
    left = moved(pack, "gx", 1)
    corner = diagonal(last)

    def slice_with_margins(k, margin):
        return jnp.stack(
            [
                jnp.concatenate([above[k], own[k]], axis=0),
                jnp.concatenate([corner[k], margin], axis=0),
            ]
        )

    even = lax.axis_index("gz") % 2 == 0
    first, final = slice_with_margins(0, left[0]), slice_with_margins(3, left[0])
    inner = swapped(jnp.where(even, final, first), "gz", 0)
    outer = swapped(jnp.where(even, first, final), "gz", 1)
    below = moved(jnp.concatenate([own[:, 0], left[:, 0]], axis=0), "gy", -1)
    edge = jnp.concatenate(
        [jnp.concatenate([above[k, :, :32], own[k, :, :32]], axis=0) for k in range(BZ)], axis=1
    )
    right = moved(edge, "gx", -1)

    shears, offsets = shear.transpose(0, 2, 1), offset.transpose(0, 2, 1)
    strips_shape = (bricks, 4 * VIEWS * 4, TILE)
    pieces, tones, cells = pl.pallas_call(
        tone_kernel,
        out_shape=shapes(strips_shape, (VIEWS, BZ, 3, TILE, TILE), (BZ, 2, EXT, TILE)),
        in_specs=[VMEM] * 8,
        out_specs=[VMEM] * 3,
        scratch_shapes=[pltpu.VMEM((4, BZ, 2, EXT, TILE), jnp.float32)],
        compiler_params=MEDIUM,
        cost_estimate=pl.CostEstimate(
            flops=10**7, bytes_accessed=4 * 10**6, transcendentals=3 * 10**6
        ),
        name="tone",
    )(shears, offsets, palette.T, rate[None], own, above, left, corner)
    (pieces,) = pl.pallas_call(
        render_kernel,
        out_shape=shapes(strips_shape),
        in_specs=[VMEM] * 10,
        out_specs=[VMEM],
        input_output_aliases={3: 0},
        scratch_shapes=[pltpu.VMEM((3, BZ, 2, EXT, TILE), jnp.float32)],
        compiler_params=MEDIUM,
        name="render",
    )(shears, offsets, light, pieces, tones, cells, inner, outer, below, right)

    strips = lax.all_to_all(pieces, "gz", 0, 0, tiled=True)

    return pl.pallas_call(
        composite_kernel,
        out_shape=jax.ShapeDtypeStruct((VIEWS, 4, 1, 4, TILE), jnp.float32),
        in_specs=[VMEM] * 2,
        out_specs=VMEM,
        compiler_params=pltpu.CompilerParams(vmem_limit_bytes=16 * 1024 * 1024),
        name="composite",
    )(order, strips)


def solution(mesh):
    return jax.shard_map(
        on_device,
        mesh=mesh,
        in_specs=(P("gz", "gy", "gx"), P(), P(), P(), P(), P(), P()),
        out_specs=P(None, None, "gz", "gy", "gx"),
        check_vma=False,
    )
```

```python
import jax
import jax.numpy as jnp
from jax import lax
from jax.experimental import pallas as pl
from jax.experimental.pallas import tpu as pltpu
from jax.sharding import PartitionSpec as P

VIEWS = 4
BZ = 4
TILE = 128
HALO = 40
EXT = HALO + TILE
CHUNK = 16

VMEM = pl.BlockSpec(memory_space=pltpu.VMEM)
MEDIUM = pltpu.CompilerParams(vmem_limit_bytes=20 * 1024 * 1024)
SMALL = pltpu.CompilerParams(vmem_limit_bytes=8 * 1024 * 1024)


def pack_kernel(own_ref, last_ref, pack_ref, copy_ref):
    lane = lax.broadcasted_iota(jnp.int32, (TILE, TILE), 1)
    last_ref[...] = own_ref[:, TILE - HALO :]
    copy_ref[...] = own_ref[...]
    for k in range(2):
        pack_ref[k] = jnp.where(
            lane < TILE // 2, pltpu.roll(own_ref[3 - k], TILE // 2, axis=1), own_ref[k]
        )


def left_margin(left_ref, k):
    return left_ref[k] if k < 2 else pltpu.roll(left_ref[3 - k], TILE // 2, axis=1)


def inside_image(base, off_r, off_c):
    shape = (CHUNK, TILE)
    rows = lax.broadcasted_iota(jnp.int32, shape, 0) + (lax.axis_index("gy") * TILE + base)
    cols = lax.broadcasted_iota(jnp.int32, shape, 1) + lax.axis_index("gx") * TILE
    return jnp.logical_and(rows >= off_r, cols >= off_c)


def moves_of(shear_ref, offset_ref):
    brick = lax.axis_index("gz")
    shear = pltpu.roll(shear_ref[...], shear_ref.shape[2] - brick * BZ, axis=2)
    offset = offset_ref[...]
    here = lax.broadcasted_iota(jnp.int32, offset.shape, 2) == brick
    place = jnp.sum(jnp.where(here, offset, 0), axis=2, keepdims=True)
    total = shear + place
    cells = [[(total[v, 0, k], total[v, 1, k]) for k in range(BZ)] for v in range(VIEWS)]
    return cells, [(place[v, 0, 0], place[v, 1, 0]) for v in range(VIEWS)]


def sampler(move, k, base):
    dy, dx = move
    rows = pl.ds(base + (HALO - dy), CHUNK)
    own = lax.broadcasted_iota(jnp.int32, (CHUNK, TILE), 1) < TILE - dx

    def sample(ref, a):
        return pltpu.roll(jnp.where(own, ref[a, k, 0, rows], ref[a, k, 1, rows]), dx, axis=1)

    return sample


def store_strips(pieces_ref, base, row, value):
    for q in range(CHUNK // 4):
        pieces_ref[base // 4 + q, row : row + 4] = value[4 * q : 4 * q + 4]


def tone_kernel(
    shear_ref, offset_ref, palette_ref, rate_ref, own_ref, above_ref, left_ref, corner_ref,
    pieces_ref, tones_ref, cells_ref,
    fields,
):
    def tone(value, k, half, rows):
        cells_ref[k, half, rows] = value
        fields[0, k, half, rows] = jnp.tanh(value)
        for c3 in range(3):
            arg = palette_ref[0, c3] + palette_ref[1, c3] * value
            fields[1 + c3, k, half, rows] = 0.5 + 0.5 * jnp.tanh(0.5 * arg)

    for k in range(BZ):
        tone(above_ref[k], k, 0, slice(0, HALO))
        tone(own_ref[k], k, 0, slice(HALO, EXT))
        tone(corner_ref[k], k, 1, slice(0, HALO))
        tone(left_margin(left_ref, k), k, 1, slice(HALO, EXT))

    moves, places = moves_of(shear_ref, offset_ref)
    for view in range(VIEWS):
        off_r, off_c = places[view]
        rate = rate_ref[0, view]
        for base in range(0, TILE, CHUNK):
            depth = jnp.zeros((CHUNK, TILE), jnp.float32)
            clear = inside_image(base, off_r, off_c).astype(jnp.float32)
            inside = clear
            for k in range(BZ):
                sample = sampler(moves[view][k], k, base)
                density = rate * (1.0 + sample(fields, 0))
                kept = clear * jnp.exp(-density)
                weight = clear - kept
                for c3 in range(3):
                    tones_ref[view, k, c3, base : base + CHUNK] = sample(fields, 1 + c3) * weight
                depth = depth + density
                clear = kept
            store_strips(pieces_ref, base, 48 + view * 4, depth * inside)


def make_normals(tiles, cells_ref, inner_ref, outer_ref, below_ref, right_ref, normals):
    lane8 = lax.broadcasted_iota(jnp.int32, (8, TILE), 1)
    row8 = lax.broadcasted_iota(jnp.int32, (8, TILE), 0)
    even = jnp.full((8, TILE), lax.axis_index("gz"), jnp.int32) % 2 == 0

    for i in tiles:
        row = slice(8 * i, 8 * i + 8)
        cells = [[cells_ref[k, half, row] for half in range(2)] for k in range(BZ)]
        inner = [inner_ref[half, row] for half in range(2)]
        outer = [outer_ref[half, row] for half in range(2)]
        front = [jnp.where(even, b, a) for b, a in zip(outer, inner, strict=True)]
        back = [jnp.where(even, a, b) for b, a in zip(outer, inner, strict=True)]
        if 8 * i >= HALO:
            front[1] = pltpu.roll(front[1], TILE // 2, axis=1)
        edge = right_ref[row]
        for k in range(BZ):
            c, s = cells[k]
            c_next = pltpu.roll(c, TILE - 1, axis=1)
            s_prev = pltpu.roll(s, 1, axis=1)
            c_right = jnp.where(
                lane8 == TILE - 1, pltpu.roll(edge, TILE - 1 - 32 * k, axis=1), c_next
            )
            c_left = jnp.where(lane8 == 0, s_prev, pltpu.roll(c, 1, axis=1))
            s_right = jnp.where(lane8 == TILE - 1, c_next, pltpu.roll(s, TILE - 1, axis=1))
            before = front if k == 0 else cells[k - 1]
            after = back if k == BZ - 1 else cells[k + 1]
            for half, (right, left) in enumerate(((c_right, c_left), (s_right, s_prev))):
                if i == 0:
                    upper = pltpu.roll(cells[k][half], 1, axis=0)
                else:
                    upper = cells_ref[k, half, 8 * i - 1 : 8 * i + 7]
                if i < EXT // 8 - 1:
                    lower = cells_ref[k, half, 8 * i + 1 : 8 * i + 9]
                else:
                    at = k if half == 0 else BZ + min(k, 3 - k)
                    last = jnp.broadcast_to(below_ref[at : at + 1], (8, TILE))
                    if half == 1 and k >= 2:
                        last = pltpu.roll(last, TILE // 2, axis=1)
                    lower = jnp.where(row8 == 7, last, pltpu.roll(cells[k][half], 7, axis=0))
                gd = 0.5 * (after[half] - before[half])
                gr = 0.5 * (lower - upper)
                gc = 0.5 * (right - left)
                factor = lax.rsqrt(gd * gd + gr * gr + gc * gc + 1.0)
                normals[0, k, half, row] = gd * factor
                normals[1, k, half, row] = gr * factor
                normals[2, k, half, row] = gc * factor


def normals_kernel(cells_ref, inner_ref, outer_ref, right_ref, normals):
    tiles = range(EXT // 8 - 1)
    make_normals(tiles, cells_ref, inner_ref, outer_ref, None, right_ref, normals)


def render_kernel(
    shear_ref, offset_ref, light_ref,
    started_ref, made_ref, tones_ref, cells_ref, inner_ref, outer_ref, below_ref, right_ref,
    pieces_ref, normals,
):
    tiles = (EXT // 8 - 1,)
    make_normals(tiles, cells_ref, inner_ref, outer_ref, below_ref, right_ref, normals)
    moves, _ = moves_of(shear_ref, offset_ref)
    for view in range(VIEWS):
        ld = jnp.full((8, TILE), light_ref[view, 0], jnp.float32)
        lr = jnp.full((8, TILE), light_ref[view, 1], jnp.float32)
        lc = jnp.full((8, TILE), light_ref[view, 2], jnp.float32)
        length = jnp.sqrt(ld * ld + lr * lr + lc * lc + 1.0)
        td, tr, tc = ((v / length)[0:1] for v in (ld, lr, lc))
        for base in range(0, TILE, CHUNK):
            color = [jnp.zeros((CHUNK, TILE), jnp.float32) for _ in range(3)]
            for k in range(BZ):
                sample = sampler(moves[view][k], k, base)
                dot = sample(normals, 0) * td + sample(normals, 1) * tr + sample(normals, 2) * tc
                shade = 0.25 + 0.75 * dot * dot
                for c3 in range(3):
                    color[c3] = color[c3] + tones_ref[view, k, c3, base : base + CHUNK] * shade
            for c3 in range(3):
                store_strips(pieces_ref, base, c3 * 16 + view * 4, color[c3])


def composite_kernel(order_ref, pieces_ref, out_ref):
    bricks = pieces_ref.shape[0]
    for view in range(VIEWS):
        cover = jnp.zeros((4, TILE), jnp.float32)
        color = [jnp.zeros((4, TILE), jnp.float32) for _ in range(3)]
        for place in range(bricks):
            brick = order_ref[view, place]
            clear = jnp.exp(-cover)
            for c3 in range(3):
                at = c3 * 16 + view * 4
                color[c3] = color[c3] + pieces_ref[brick, at : at + 4] * clear
            at = 48 + view * 4
            cover = cover + pieces_ref[brick, at : at + 4]
        for c3 in range(3):
            out_ref[view, c3, 0] = color[c3]
        out_ref[view, 3, 0] = 1.0 - jnp.exp(-cover)


def moved(value, axes, steps):
    count = lax.axis_size(axes)
    first, last = max(0, -steps), min(count, count - steps)
    return lax.ppermute(value, axes, [(i, i + steps) for i in range(first, last)])


def swapped(value, axis, first):
    lows = range(first, lax.axis_size(axis) - 1, 2)
    return lax.ppermute(value, axis, [p for i in lows for p in ((i, i + 1), (i + 1, i))])


def diagonal(value):
    n_y, n_x = lax.axis_size("gy"), lax.axis_size("gx")
    pairs = [
        (y * n_x + x, (y + 1) * n_x + x + 1) for y in range(n_y - 1) for x in range(n_x - 1)
    ]
    return lax.ppermute(value, ("gy", "gx"), pairs)


def on_device(pressure, light, palette, rate, shear, offset, order):
    bricks = order.shape[1]

    def shapes(*dims):
        return [jax.ShapeDtypeStruct(dim, jnp.float32) for dim in dims]

    last, pack, own = pl.pallas_call(
        pack_kernel,
        out_shape=shapes((BZ, HALO, TILE), (2, TILE, TILE), (BZ, TILE, TILE)),
        in_specs=[VMEM],
        out_specs=[VMEM] * 3,
        compiler_params=SMALL,
        name="pack",
    )(pressure)
    above = moved(last, "gy", 1)
    left = moved(pack, "gx", 1)
    corner = diagonal(last)

    def slice_with_margins(k, margin):
        return jnp.stack(
            [
                jnp.concatenate([above[k], own[k]], axis=0),
                jnp.concatenate([corner[k], margin], axis=0),
            ]
        )

    even = lax.axis_index("gz") % 2 == 0
    first, final = slice_with_margins(0, left[0]), slice_with_margins(3, left[0])
    inner = swapped(jnp.where(even, final, first), "gz", 0)
    outer = swapped(jnp.where(even, first, final), "gz", 1)
    below = moved(jnp.concatenate([own[:, 0], left[:, 0]], axis=0), "gy", -1)
    edge = jnp.concatenate(
        [jnp.concatenate([above[k, :, :32], own[k, :, :32]], axis=0) for k in range(BZ)], axis=1
    )
    right = moved(edge, "gx", -1)

    shears, offsets = shear.transpose(0, 2, 1), offset.transpose(0, 2, 1)
    strips_shape = (bricks, 4 * VIEWS * 4, TILE)
    pieces, tones, cells = pl.pallas_call(
        tone_kernel,
        out_shape=shapes(strips_shape, (VIEWS, BZ, 3, TILE, TILE), (BZ, 2, EXT, TILE)),
        in_specs=[VMEM] * 8,
        out_specs=[VMEM] * 3,
        scratch_shapes=[pltpu.VMEM((4, BZ, 2, EXT, TILE), jnp.float32)],
        compiler_params=MEDIUM,
        cost_estimate=pl.CostEstimate(
            flops=10**7, bytes_accessed=4 * 10**6, transcendentals=3 * 10**6
        ),
        name="tone",
    )(shears, offsets, palette.T, rate[None], own, above, left, corner)
    normals_shape = (3, BZ, 2, EXT, TILE)
    (normals,) = pl.pallas_call(
        normals_kernel,
        out_shape=shapes(normals_shape),
        in_specs=[VMEM] * 4,
        out_specs=[VMEM],
        compiler_params=SMALL,
        cost_estimate=pl.CostEstimate(flops=10**7, bytes_accessed=4 * 10**6, transcendentals=10**6),
        name="normals",
    )(cells, inner, outer, right)
    pieces, _ = pl.pallas_call(
        render_kernel,
        out_shape=shapes(strips_shape, normals_shape),
        in_specs=[VMEM] * 11,
        out_specs=[VMEM] * 2,
        input_output_aliases={3: 0, 4: 1},
        compiler_params=MEDIUM,
        name="render",
    )(shears, offsets, light, pieces, normals, tones, cells, inner, outer, below, right)

    strips = lax.all_to_all(pieces, "gz", 0, 0, tiled=True)

    return pl.pallas_call(
        composite_kernel,
        out_shape=jax.ShapeDtypeStruct((VIEWS, 4, 1, 4, TILE), jnp.float32),
        in_specs=[VMEM] * 2,
        out_specs=VMEM,
        compiler_params=pltpu.CompilerParams(vmem_limit_bytes=16 * 1024 * 1024),
        name="composite",
    )(order, strips)


def solution(mesh):
    return jax.shard_map(
        on_device,
        mesh=mesh,
        in_specs=(P("gz", "gy", "gx"), P(), P(), P(), P(), P(), P()),
        out_specs=P(None, None, "gz", "gy", "gx"),
        check_vma=False,
    )
```
